32 devices in a mesh: blk: 32 (over z, y, x, core).
Axes of the slice: x: 2, y: 2, z: 4, core: 2. Of those that a mesh axis runs over, the one named last changes fastest.
Arguments:
- rhs: float32 [32768, 256], P('blk'), may hold values from -6 to 6
- diag_inv: float32 [32768, 128], P('blk')
- factor_blocks: float32 [960, 128, 128], P('blk'), may hold values from -0.125 to 0.125
- order: int32 [256], P('blk'), may hold values from 0 to 7, as said below
- blk_row: int32 [960], P('blk'), may hold values from 0 to 255, as said below
- blk_col: int32 [960], P('blk'), may hold values from 0 to 255, as said below
Outputs:
- solution: float32 [32768, 256], P('blk')
The draws below stay inside these ranges and needn't reach their ends.
Inputs may be any that keep to these rules, and one draw needn't show every extreme that they name: `order`: for each device d, entries d * 8 to d * 8 + 7 are a permutation of 0 to 7. `blk_row`: stored block j lies on device j // 30; with p = j % 30 and k = p // 10, its row is a block row of that same device whose level is above k. `blk_col`: with j, p and k as for blk_row and e = (p // 2) % 5, the 2 blocks that share j // 30, k and e have as columns, each once, the 2 block rows of level k of the device e places below j // 30, counted cyclically over all devices.
All inputs are finite; a program needn't handle non-finite values.
Results may differ from the reference program's by a relative error of at most 0.0001.
Values sent between devices are 32-bit elements; how exact they have to be, the bound alone decides.
A program may use at most 64 MiB of HBM per device.

```python
import math
import jax
import jax.numpy as jnp
from jax import lax

BS = 128
RHS = 256
LANES = 2
STEPS = 4
BAND = 4
R = 8
NOFF = 30
NB = 256
NROWS = 32768
N_BLK = 32


def pattern(key):
    perm_keys = jax.random.split(jax.random.fold_in(key, 11), N_BLK)
    orders = jax.vmap(lambda single: jax.random.permutation(single, R))(perm_keys).astype(jnp.int32)
    indices = jnp.arange(NOFF, dtype=jnp.int32)
    step_of = indices // ((BAND + 1) * LANES)
    offset_of = indices // LANES % (BAND + 1)
    lane_of = indices % LANES
    devices = jnp.arange(N_BLK, dtype=jnp.int32)[:, None]
    owners = (devices - offset_of[None, :]) % N_BLK
    col_slot = orders[owners, (step_of * LANES + lane_of)[None, :]]
    columns = owners * R + col_slot
    spread = (STEPS - 1 - step_of)[None, :]
    row_level = jax.random.randint(jax.random.fold_in(key, 12), (N_BLK, NOFF), 0, 1 << 20) % spread + step_of[None, :] + 1
    row_lane = jax.random.randint(jax.random.fold_in(key, 13), (N_BLK, NOFF), 0, LANES)
    row_slot = jnp.take_along_axis(orders, row_level * LANES + row_lane, axis=1)
    rows_out = devices * R + row_slot
    return (orders.reshape(-1), rows_out.reshape(-1).astype(jnp.int32), columns.reshape(-1).astype(jnp.int32))


def draw_order(key, part):
    return pattern(key)[0]


def draw_blk_row(key, part):
    return pattern(key)[1]


def draw_blk_col(key, part):
    return pattern(key)[2]


def draw_diag_inv(key, part):
    row_index = jnp.arange(NB * BS, dtype=jnp.int32) % BS
    identity = (row_index[:, None] == jnp.arange(BS, dtype=jnp.int32)[None, :]).astype(jnp.float32)
    noise_part = jax.random.normal(key, (NB * BS, BS), jnp.float32) * (0.5 / math.sqrt(BS))
    return identity + noise_part


def steps_of(rng, shape, cuts, least, top_value):
    loudness, own = 1.0, jax.random.fold_in(rng, 6)
    for axis_at, blocks in cuts:
        draws = jnp.exp(jax.random.uniform(jax.random.fold_in(own, axis_at), (blocks,), jnp.float32, least / len(cuts), top_value / len(cuts)))
        loudness = loudness * jnp.repeat(draws, shape[axis_at] // blocks).reshape([-1 if axis == axis_at else 1 for axis in range(len(shape))])
    return loudness


def scatter_about(key, dims, scale, reach, cuts=(), kind=jnp.bfloat16):
    gain = steps_of(key, dims, cuts, -0.22, 0.18) if cuts else 1.0
    array = jax.random.normal(key, dims, jnp.float32) * scale * gain
    return jnp.minimum(jnp.maximum(array, -reach), reach).astype(kind)


def setup_inputs(seed: int = 0) -> dict:
    streams_of = jax.random.split(jax.random.key(seed), 7)
    return {
        "rhs": scatter_about(streams_of[0], (NROWS, RHS), 1.0, 6.0, ((0, 32),), jnp.float32),
        "diag_inv": draw_diag_inv(jax.random.fold_in(streams_of[6], 71), 0),
        "factor_blocks": scatter_about(streams_of[2], (NOFF * N_BLK, BS, BS), (16 * BS) ** -0.5, 0.125, ((0, 32),), jnp.float32),
        "order": draw_order(jax.random.fold_in(streams_of[6], 71), 0),
        "blk_row": draw_blk_row(jax.random.fold_in(streams_of[6], 71), 0),
        "blk_col": draw_blk_col(jax.random.fold_in(streams_of[6], 71), 0),
    }


def reference(rhs, diag_inv, factor_blocks, order, blk_row, blk_col):
    block_rows = rhs.reshape(NB, BS, RHS)
    inverses = diag_inv.reshape(NB, BS, BS)
    positions = jnp.arange(NB, dtype=jnp.int32)
    owners = positions // R
    level_at = ((positions % R) // LANES).astype(jnp.int32)
    levels = jnp.zeros((NB,), jnp.int32).at[owners * R + order.astype(jnp.int32)].set(level_at)
    residual = block_rows.astype(jnp.float32)
    solution = jnp.zeros((NB, BS, RHS), jnp.float32)
    column_levels = levels[blk_col]
    for step_index in range(STEPS):
        rows_now = jnp.nonzero(levels == step_index, size=N_BLK * LANES)[0].astype(jnp.int32)
        solved = jnp.einsum("nij,njc->nic", inverses[rows_now], residual[rows_now], precision=lax.Precision.HIGHEST)
        solution = solution.at[rows_now].set(solved)
        if step_index + 1 < STEPS:
            chosen = jnp.nonzero(column_levels == step_index, size=N_BLK * (BAND + 1) * LANES)[0].astype(jnp.int32)
            chosen = chosen.reshape(BAND + 1, N_BLK * LANES)

            def apply_group(carried, picked):
                contribution = jnp.einsum("nij,njc->nic", factor_blocks[picked], solution[blk_col[picked]], precision=lax.Precision.HIGHEST)
                return carried.at[blk_row[picked]].add(-contribution), None

            residual, _ = lax.scan(apply_group, residual, chosen)
    return solution.reshape(NROWS, RHS)
```

```python
import functools

import jax
import jax.numpy as jnp
from jax import lax
from jax.experimental import pallas as pl
from jax.experimental.pallas import tpu as pltpu
from jax.sharding import PartitionSpec as P

LANES = 2
STEPS = 4
BAND = 4
PARTS = 2
GROUPS = BAND + 1
MESH = pl.DeviceIdType.MESH
F32 = jnp.float32
BF16 = jnp.bfloat16


def split(x):
    high = x.astype(BF16)
    return high, (x - high.astype(F32)).astype(BF16)


def dot(a, b):
    return jnp.dot(a, b, preferred_element_type=F32)


def kernel(
    n,
    order_ref,
    row_ref,
    col_ref,
    rhs_hbm,
    diag_hbm,
    factor_hbm,
    out_ref,
    rhs_ref,
    diag_ref,
    factor_ref,
    diag_hi,
    diag_lo,
    a_hi,
    a_lo,
    acc,
    own,
    got,
    xcat,
    load_sems,
    send_sems,
    recv_sems,
):
    slots = order_ref.shape[0]
    size = diag_ref.shape[1]
    width = rhs_ref.shape[2] // PARTS
    me = lax.axis_index("blk")
    core = lax.rem(me, 2)
    chip = me // 2
    odd = lax.rem(chip, 2)
    partner = me + 1 - 2 * core
    buddy = me + 2 - 4 * odd
    above = lax.rem(me + 4, n)
    below = lax.rem(me + n - 4, n)

    loads = [
        pltpu.make_async_copy(src, dst, load_sems.at[at])
        for at, (src, dst) in enumerate(
            ((diag_hbm, diag_ref), (rhs_hbm, rhs_ref), (factor_hbm, factor_ref))
        )
    ]
    for load in loads:
        load.start()

    barrier = pltpu.get_barrier_semaphore()
    for device in (partner, buddy, below):
        pl.semaphore_signal(barrier, inc=1, device_id=(device,), device_id_type=MESH)
    pl.semaphore_wait(barrier, 3)

    slot_at = []
    for level in range(STEPS):
        one, two = order_ref[2 * level], order_ref[2 * level + 1]
        slot_at += [jnp.minimum(one, two), jnp.maximum(one, two)]

    def lane(m):
        return pl.ds(m * size, size)

    def own_at(level, part, m):
        return (part * STEPS + level) * LANES + m

    def copy(t, m, kind, src, entry, device):
        at = (t * LANES + m) * 4
        return pltpu.make_async_remote_copy(
            src_ref=src,
            dst_ref=got.at[t, entry - 1].at[lane(m)],
            send_sem=send_sems.at[at + kind],
            recv_sem=recv_sems.at[at + entry - 1],
            device_id=(device,),
            device_id_type=MESH,
        )

    def mine(t, m):
        return own.at[own_at(t // PARTS, lax.rem(t, PARTS), m)]

    def there(t, m, entry):
        return got.at[t, entry - 1].at[lane(m)]

    def send_own(t, m):
        copy(t, m, 0, mine(t, m), 4, above).start()

        @pl.when(odd == 0)
        def _():
            copy(t, m, 1, mine(t, m), 2, buddy).start()

        @pl.when(core == 0)
        def _():
            copy(t, m, 3, mine(t, m), 1, partner).start()

    def take_far(t, m):
        copy(t, m, 0, mine(t, m), 4, above).wait_recv()

        @pl.when(odd == 1)
        def _():
            copy(t, m, 1, there(t, m, 4), 2, buddy).start()

        @pl.when(core == 1)
        def _():
            copy(t, m, 3, there(t, m, 4), 3, partner).start()

    def take_near(t, m):
        copy(t, m, 1, mine(t, m), 2, buddy).wait_recv()
        copy(t, m, 2, there(t, m, 2), 3 - 2 * core, partner).start()

    def take_other(t, m, entry):
        copy(t, m, 2, mine(t, m), entry, partner).wait_recv()

    def put(entry, x):
        high, low = split(x)
        xcat[entry, :, 0:width] = high
        xcat[entry, :, width:] = low

    def product(k, level, entry):
        at = k * (STEPS - 1) + level - 1
        wide = dot(a_hi[at, entry], xcat[entry])
        small = dot(a_lo[at, entry], xcat[entry, :, 0:width])
        return wide[:, 0:width] + wide[:, width:] + small

    def solve(level, part, residual, send):
        t = level * PARTS + part
        for m in range(LANES):
            high, low = split(residual[m * size : (m + 1) * size])
            both = jnp.concatenate([high, low], axis=1)
            wide = dot(diag_hi[level * LANES + m], both)
            small = dot(diag_lo[level * LANES + m], high)
            own[own_at(level, part, m)] = wide[:, 0:width] + wide[:, width:] + small
            send(t, m)

    def assemble(k):
        def one(index, carry):
            entry, c = index // LANES, lax.rem(index, LANES)
            base = k * GROUPS * LANES + entry * LANES
            swapped = (col_ref[base] > col_ref[base + 1]).astype(jnp.int32)
            second = swapped + c - 2 * swapped * c
            high, low = split(factor_ref[base + second])
            high, low = high.astype(F32), low.astype(F32)
            slot = row_ref[base] * (1 - second) + row_ref[base + 1] * second - me * slots
            columns = pl.ds(pl.multiple_of(c * size, size), size)
            for level in range(k + 1, STEPS):
                at = k * (STEPS - 1) + level - 1
                for m in range(LANES):
                    here = (slot == slot_at[level * LANES + m]).astype(jnp.int32).astype(F32)
                    rows = pl.ds(m * size, size)
                    a_hi[at, entry, rows, columns] = (high * here).astype(BF16)
                    a_lo[at, entry, rows, columns] = (low * here).astype(BF16)
            return carry

        lax.fori_loop(0, GROUPS * LANES, one, 0)

    loads[0].wait()
    for p in range(slots):
        high, low = split(diag_ref[slot_at[p]])
        diag_hi[p] = high
        diag_lo[p] = low
    loads[1].wait()

    def rhs_of(level, part):
        columns = slice(part * width, (part + 1) * width)
        rows = [rhs_ref[slot_at[level * LANES + m]][:, columns] for m in range(LANES)]
        return jnp.concatenate(rows, axis=0)

    for part in range(PARTS):
        solve(0, part, rhs_of(0, part), send_own)
    for level in range(1, STEPS):
        for part in range(PARTS):
            acc[level * PARTS + part] = rhs_of(level, part)
    loads[2].wait()
    assemble(0)

    def step(t, carry):
        k, part = t // PARTS, lax.rem(t, PARTS)
        ahead = k + 1
        put(0, jnp.concatenate([own[own_at(k, part, m)] for m in range(LANES)], axis=0))
        for m in range(LANES):
            take_far(t, m)
        for m in range(LANES):
            take_near(t, m)
        residual = acc[ahead * PARTS + part] - product(k, ahead, 0)
        for entry in (4, 2):
            put(entry, got[t, entry - 1])
            residual = residual - product(k, ahead, entry)
        for entry in (1, 3):
            for m in range(LANES):
                take_other(t, m, entry)
            put(entry, got[t, entry - 1])
            residual = residual - product(k, ahead, entry)

        def send(where, m):
            @pl.when(ahead < STEPS - 1)
            def _():
                send_own(where, m)

        solve(ahead, part, residual, send)

        def later(level, inner):
            total = product(k, level, 0)
            for entry in range(1, GROUPS):
                total = total + product(k, level, entry)
            acc[level * PARTS + part] = acc[level * PARTS + part] - total
            return inner

        lax.fori_loop(k + 2, STEPS, later, 0)
        for done in range(STEPS - 2):

            @pl.when(t == done * PARTS + PARTS - 1)
            def _():
                assemble(done + 1)

        return carry

    lax.fori_loop(0, (STEPS - 1) * PARTS, step, 0)

    for slot in range(slots):
        position = jnp.int32(0)
        for p in range(slots):
            position = position + p * (slot_at[p] == slot).astype(jnp.int32)
        for part in range(PARTS):
            out_ref[slot * size : (slot + 1) * size, part * width : (part + 1) * width] = own[
                part * slots + jnp.minimum(position, slots - 1)
            ]

    def finish(t, carry):
        for m in range(LANES):
            for kind in range(4):
                copy(t, m, kind, mine(t, m), 1, partner).wait_send()
        return carry

    lax.fori_loop(0, (STEPS - 1) * PARTS, finish, 0)


def body(rhs, diag_inv, factor_blocks, order, blk_row, blk_col):
    n = lax.axis_size("blk")
    rows, columns = rhs.shape
    size = diag_inv.shape[1]
    slots = order.shape[0]
    pairs = (STEPS - 1) * (STEPS - 1)
    width = columns // PARTS
    two = LANES * size
    rounds = (STEPS - 1) * PARTS
    scratch = [
        pltpu.VMEM((slots, size, columns), F32),
        pltpu.VMEM((slots, size, size), F32),
        pltpu.VMEM(factor_blocks.shape, F32),
        pltpu.VMEM((slots, size, size), BF16),
        pltpu.VMEM((slots, size, size), BF16),
        pltpu.VMEM((pairs, GROUPS, two, two), BF16),
        pltpu.VMEM((pairs, GROUPS, two, two), BF16),
        pltpu.VMEM((STEPS * PARTS, two, width), F32),
        pltpu.VMEM((PARTS * slots, size, width), F32),
        pltpu.VMEM((rounds, BAND, two, width), F32),
        pltpu.VMEM((GROUPS, two, PARTS * width), BF16),
        pltpu.SemaphoreType.DMA((3,)),
        pltpu.SemaphoreType.DMA((rounds * LANES * 4,)),
        pltpu.SemaphoreType.DMA((rounds * LANES * 4,)),
    ]
    return pl.pallas_call(
        functools.partial(kernel, n),
        out_shape=jax.ShapeDtypeStruct(rhs.shape, F32),
        in_specs=[pl.BlockSpec(memory_space=pltpu.SMEM)] * 3
        + [pl.BlockSpec(memory_space=pl.ANY)] * 3,
        out_specs=pl.BlockSpec(memory_space=pltpu.VMEM),
        scratch_shapes=scratch,
        compiler_params=pltpu.CompilerParams(
            collective_id=0, has_side_effects=True, vmem_limit_bytes=56 * 1024 * 1024
        ),
        cost_estimate=pl.CostEstimate(
            flops=2 * 3 * (factor_blocks.shape[0] + slots) * size * size * columns,
            bytes_accessed=4 * (2 * rows * columns + rows * size + factor_blocks.size),
            transcendentals=0,
        ),
    )(
        order,
        blk_row,
        blk_col,
        rhs.reshape(slots, size, columns),
        diag_inv.reshape(slots, size, size),
        factor_blocks,
    )


def solution(mesh):
    placed = (P("blk", None), P("blk", None), P("blk", None, None), P("blk"), P("blk"), P("blk"))
    return jax.shard_map(
        body, mesh=mesh, in_specs=placed, out_specs=P("blk", None), check_vma=False
    )
```

```python
import functools

import jax
import jax.numpy as jnp
from jax import lax
from jax.experimental import pallas as pl
from jax.experimental.pallas import tpu as pltpu
from jax.sharding import PartitionSpec as P

LANES = 2
STEPS = 4
BAND = 4
PARTS = 2
GROUPS = BAND + 1
MESH = pl.DeviceIdType.MESH
F32 = jnp.float32
BF16 = jnp.bfloat16


def split(x):
    high = x.astype(BF16)
    return high, (x - high.astype(F32)).astype(BF16)


def dot(a, b):
    return jnp.dot(a, b, preferred_element_type=F32)


def kernel(
    n,
    order_ref,
    row_ref,
    col_ref,
    rhs_hbm,
    diag_hbm,
    factor_hbm,
    out_ref,
    rhs_ref,
    diag_ref,
    factor_ref,
    diag_two,
    factor_two,
    where_to,
    acc,
    own,
    got,
    terms,
    load_sems,
    send_sems,
    recv_sems,
):
    slots = order_ref.shape[0]
    size = diag_ref.shape[1]
    width = rhs_ref.shape[2] // PARTS
    me = lax.axis_index("blk")
    core = lax.rem(me, 2)
    chip = me // 2
    odd = lax.rem(chip, 2)
    partner = me + 1 - 2 * core
    buddy = me + 2 - 4 * odd
    above = lax.rem(me + 4, n)
    below = lax.rem(me + n - 4, n)

    loads = [
        pltpu.make_async_copy(src, dst, load_sems.at[at])
        for at, (src, dst) in enumerate(
            ((diag_hbm, diag_ref), (rhs_hbm, rhs_ref), (factor_hbm, factor_ref))
        )
    ]
    for load in loads:
        load.start()

    barrier = pltpu.get_barrier_semaphore()
    for device in (partner, buddy, below):
        pl.semaphore_signal(barrier, inc=1, device_id=(device,), device_id_type=MESH)
    pl.semaphore_wait(barrier, 3)

    slot_at = []
    for level in range(STEPS):
        one, two = order_ref[2 * level], order_ref[2 * level + 1]
        slot_at += [jnp.minimum(one, two), jnp.maximum(one, two)]

    def lane(m):
        return pl.ds(m * size, size)

    def own_at(level, part, m):
        return (part * STEPS + level) * LANES + m

    def copy(t, m, kind, src, entry, device):
        at = (t * LANES + m) * 4
        return pltpu.make_async_remote_copy(
            src_ref=src,
            dst_ref=got.at[t, entry - 1].at[lane(m)],
            send_sem=send_sems.at[at + kind],
            recv_sem=recv_sems.at[at + entry - 1],
            device_id=(device,),
            device_id_type=MESH,
        )

    def mine(t, m):
        return own.at[own_at(t // PARTS, lax.rem(t, PARTS), m)]

    def there(t, m, entry):
        return got.at[t, entry - 1].at[lane(m)]

    def send_own(t, m):
        copy(t, m, 0, mine(t, m), 4, above).start()

        @pl.when(odd == 0)
        def _():
            copy(t, m, 1, mine(t, m), 2, buddy).start()

        @pl.when(core == 0)
        def _():
            copy(t, m, 3, mine(t, m), 1, partner).start()

    def take_far(t, m):
        copy(t, m, 0, mine(t, m), 4, above).wait_recv()

        @pl.when(odd == 1)
        def _():
            copy(t, m, 1, there(t, m, 4), 2, buddy).start()

        @pl.when(core == 1)
        def _():
            copy(t, m, 3, there(t, m, 4), 3, partner).start()

    def take_near(t, m):
        copy(t, m, 1, mine(t, m), 2, buddy).wait_recv()
        copy(t, m, 2, there(t, m, 2), 3 - 2 * core, partner).start()

    def take_other(t, m, entry):
        copy(t, m, 2, mine(t, m), entry, partner).wait_recv()

    def tall(x):
        return jnp.concatenate(split(x), axis=0)

    def multiply(two, x):
        every = dot(two, jnp.concatenate(split(x), axis=1))
        top = every[0:size, 0:width] + every[0:size, width:]
        return top + (every[size:, 0:width] + every[size:, width:])

    def solve(level, part, residual, send):
        t = level * PARTS + part
        for m in range(LANES):
            own[own_at(level, part, m)] = multiply(diag_two[level * LANES + m], residual[m])
            send(t, m)

    def prepare(index, carry):
        c = lax.rem(index, LANES)
        base = index - c
        swapped = (col_ref[base] > col_ref[base + 1]).astype(jnp.int32)
        second = swapped + c - 2 * swapped * c
        factor_two[index] = tall(factor_ref[base + second])
        slot = row_ref[base] * (1 - second) + row_ref[base + 1] * second - me * slots
        position = jnp.int32(0)
        for p in range(slots):
            position = position + p * (slot_at[p] == slot).astype(jnp.int32)
        where_to[index] = position
        return carry

    def weight(j, position):
        return (where_to[j] == position).astype(jnp.int32).astype(F32)

    loads[0].wait()
    for p in range(slots):
        diag_two[p] = tall(diag_ref[slot_at[p]])
    loads[1].wait()

    def rhs_of(level, part):
        columns = slice(part * width, (part + 1) * width)
        return [rhs_ref[slot_at[level * LANES + m]][:, columns] for m in range(LANES)]

    for part in range(PARTS):
        solve(0, part, rhs_of(0, part), send_own)
    for level in range(1, STEPS):
        for part in range(PARTS):
            for m, block in enumerate(rhs_of(level, part)):
                acc[own_at(level, part, m)] = block
    loads[2].wait()
    lax.fori_loop(0, (STEPS - 1) * GROUPS * LANES, prepare, 0)

    def step(t, carry):
        k, part = t // PARTS, lax.rem(t, PARTS)
        ahead = k + 1
        first = k * GROUPS * LANES
        residual = [acc[own_at(ahead, part, m)] for m in range(LANES)]

        def use(entry, c, x):
            j = entry * LANES + c
            term = multiply(factor_two[first + j], x)
            terms[j] = term
            for m in range(LANES):
                residual[m] = residual[m] - weight(first + j, ahead * LANES + m) * term

        for m in range(LANES):
            use(0, m, own[own_at(k, part, m)])
        for m in range(LANES):
            take_far(t, m)
        for m in range(LANES):
            take_near(t, m)
        for entry in (4, 2):
            for m in range(LANES):
                use(entry, m, got[t, entry - 1, lane(m), :])
        for m in range(LANES):
            for entry in (1, 3):
                take_other(t, m, entry)
                use(entry, m, got[t, entry - 1, lane(m), :])

        def send(where, m):
            @pl.when(ahead < STEPS - 1)
            def _():
                send_own(where, m)

        solve(ahead, part, residual, send)

        def later(level, inner):
            for m in range(LANES):
                total = acc[own_at(level, part, m)]
                for j in range(GROUPS * LANES):
                    total = total - weight(first + j, level * LANES + m) * terms[j]
                acc[own_at(level, part, m)] = total
            return inner

        lax.fori_loop(k + 2, STEPS, later, 0)
        return carry

    lax.fori_loop(0, (STEPS - 1) * PARTS, step, 0)

    for slot in range(slots):
        position = jnp.int32(0)
        for p in range(slots):
            position = position + p * (slot_at[p] == slot).astype(jnp.int32)
        for part in range(PARTS):
            out_ref[part, slot * size : (slot + 1) * size, :] = own[
                part * slots + jnp.minimum(position, slots - 1)
            ]

    def finish(t, carry):
        for m in range(LANES):
            for kind in range(4):
                copy(t, m, kind, mine(t, m), 1, partner).wait_send()
        return carry

    lax.fori_loop(0, (STEPS - 1) * PARTS, finish, 0)


def body(rhs, diag_inv, factor_blocks, order, blk_row, blk_col):
    n = lax.axis_size("blk")
    rows, columns = rhs.shape
    size = diag_inv.shape[1]
    slots = order.shape[0]
    width = columns // PARTS
    two = LANES * size
    rounds = (STEPS - 1) * PARTS
    scratch = [
        pltpu.VMEM((slots, size, columns), F32),
        pltpu.VMEM((slots, size, size), F32),
        pltpu.VMEM(factor_blocks.shape, F32),
        pltpu.VMEM((slots, two, size), BF16),
        pltpu.VMEM((factor_blocks.shape[0], two, size), BF16),
        pltpu.SMEM((factor_blocks.shape[0],), jnp.int32),
        pltpu.VMEM((PARTS * slots, size, width), F32),
        pltpu.VMEM((PARTS * slots, size, width), F32),
        pltpu.VMEM((rounds, BAND, two, width), F32),
        pltpu.VMEM((GROUPS * LANES, size, width), F32),
        pltpu.SemaphoreType.DMA((3,)),
        pltpu.SemaphoreType.DMA((rounds * LANES * 4,)),
        pltpu.SemaphoreType.DMA((rounds * LANES * 4,)),
    ]
    halves = pl.pallas_call(
        functools.partial(kernel, n),
        out_shape=jax.ShapeDtypeStruct((PARTS, rows, width), F32),
        in_specs=[pl.BlockSpec(memory_space=pltpu.SMEM)] * 3
        + [pl.BlockSpec(memory_space=pl.ANY)] * 3,
        out_specs=pl.BlockSpec(memory_space=pltpu.VMEM),
        scratch_shapes=scratch,
        compiler_params=pltpu.CompilerParams(
            collective_id=0, has_side_effects=True, vmem_limit_bytes=56 * 1024 * 1024
        ),
        cost_estimate=pl.CostEstimate(
            flops=2 * 3 * (factor_blocks.shape[0] + slots) * size * size * columns,
            bytes_accessed=4 * (2 * rows * columns + rows * size + factor_blocks.size),
            transcendentals=0,
        ),
    )(
        order,
        blk_row,
        blk_col,
        rhs.reshape(slots, size, columns),
        diag_inv.reshape(slots, size, size),
        factor_blocks,
    )
    return jnp.concatenate([halves[part] for part in range(PARTS)], axis=1)


def solution(mesh):
    placed = (P("blk", None), P("blk", None), P("blk", None, None), P("blk"), P("blk"), P("blk"))
    return jax.shard_map(
        body, mesh=mesh, in_specs=placed, out_specs=P("blk", None), check_vma=False
    )
```

```python
import functools

import jax
import jax.numpy as jnp
from jax import lax
from jax.experimental import pallas as pl
from jax.experimental.pallas import tpu as pltpu
from jax.sharding import PartitionSpec as P

LANES = 2
STEPS = 4
BAND = 4
PARTS = 2
GROUPS = BAND + 1
MESH = pl.DeviceIdType.MESH
F32 = jnp.float32
BF16 = jnp.bfloat16


def split(x):
    high = x.astype(BF16)
    return high, (x - high.astype(F32)).astype(BF16)


def dot(a, b):
    return jnp.dot(a, b, preferred_element_type=F32)


def kernel(
    n,
    order_ref,
    row_ref,
    col_ref,
    rhs_hbm,
    diag_hbm,
    factor_hbm,
    out_hbm,
    rhs_ref,
    diag_ref,
    factor_ref,
    diag_two,
    factor_two,
    where_to,
    acc,
    own,
    got,
    terms,
    load_sems,
    out_sems,
    send_sems,
    recv_sems,
):
    slots = order_ref.shape[0]
    size = diag_ref.shape[1]
    width = rhs_ref.shape[2] // PARTS
    me = lax.axis_index("blk")
    core = lax.rem(me, 2)
    chip = me // 2
    odd = lax.rem(chip, 2)
    partner = me + 1 - 2 * core
    buddy = me + 2 - 4 * odd
    above = lax.rem(me + 4, n)
    below = lax.rem(me + n - 4, n)

    loads = [
        pltpu.make_async_copy(src, dst, load_sems.at[at])
        for at, (src, dst) in enumerate(
            ((diag_hbm, diag_ref), (rhs_hbm, rhs_ref), (factor_hbm, factor_ref))
        )
    ]
    for load in loads:
        load.start()

    barrier = pltpu.get_barrier_semaphore()
    for device in (partner, buddy, below):
        pl.semaphore_signal(barrier, inc=1, device_id=(device,), device_id_type=MESH)
    pl.semaphore_wait(barrier, 3)

    slot_at = []
    for level in range(STEPS):
        one, two = order_ref[2 * level], order_ref[2 * level + 1]
        slot_at += [jnp.minimum(one, two), jnp.maximum(one, two)]

    def lane(m):
        return pl.ds(m * size, size)

    def own_at(level, part, m):
        return (part * STEPS + level) * LANES + m

    def copy(t, m, kind, src, entry, device):
        at = (t * LANES + m) * 4
        return pltpu.make_async_remote_copy(
            src_ref=src,
            dst_ref=got.at[t, entry - 1].at[lane(m)],
            send_sem=send_sems.at[at + kind],
            recv_sem=recv_sems.at[at + entry - 1],
            device_id=(device,),
            device_id_type=MESH,
        )

    def mine(t, m):
        return own.at[own_at(t // PARTS, lax.rem(t, PARTS), m)]

    def there(t, m, entry):
        return got.at[t, entry - 1].at[lane(m)]

    def send_own(t, m):
        copy(t, m, 0, mine(t, m), 4, above).start()

        @pl.when(odd == 0)
        def _():
            copy(t, m, 1, mine(t, m), 2, buddy).start()

        @pl.when(core == 0)
        def _():
            copy(t, m, 3, mine(t, m), 1, partner).start()

    def save(at):
        return pltpu.make_async_copy(own.at[at], out_hbm.at[at], out_sems.at[at])

    def take_far(t, m):
        copy(t, m, 0, mine(t, m), 4, above).wait_recv()

        @pl.when(odd == 1)
        def _():
            copy(t, m, 1, there(t, m, 4), 2, buddy).start()

        @pl.when(core == 1)
        def _():
            copy(t, m, 3, there(t, m, 4), 3, partner).start()

    def sent(t):
        for m in range(LANES):
            copy(t, m, 0, mine(t, m), 4, above).wait_send()

    def take_near(t, m):
        copy(t, m, 1, mine(t, m), 2, buddy).wait_recv()
        copy(t, m, 2, there(t, m, 2), 3 - 2 * core, partner).start()

    def take_other(t, m, entry):
        copy(t, m, 2, mine(t, m), entry, partner).wait_recv()

    def tall(x):
        return jnp.concatenate(split(x), axis=0)

    def multiply(two, x):
        every = dot(two, jnp.concatenate(split(x), axis=1))
        top = every[0:size, 0:width] + every[0:size, width:]
        return top + (every[size:, 0:width] + every[size:, width:])

    def solve(level, part, residual, send):
        t = level * PARTS + part
        for m in range(LANES):
            at = own_at(level, part, m)
            own[at] = multiply(diag_two[level * LANES + m], residual[m])
            send(t, m)
            save(at).start()

    def prepare(index, carry):
        c = lax.rem(index, LANES)
        base = index - c
        swapped = (col_ref[base] > col_ref[base + 1]).astype(jnp.int32)
        second = swapped + c - 2 * swapped * c
        factor_two[index] = tall(factor_ref[base + second])
        slot = row_ref[base] * (1 - second) + row_ref[base + 1] * second - me * slots
        position = jnp.int32(0)
        for p in range(slots):
            position = position + p * (slot_at[p] == slot).astype(jnp.int32)
        where_to[index] = position
        return carry

    def weight(j, position):
        return (where_to[j] == position).astype(jnp.int32).astype(F32)

    loads[0].wait()
    for p in range(slots):
        diag_two[p] = tall(diag_ref[slot_at[p]])
    loads[1].wait()

    def rhs_of(level, part):
        columns = slice(part * width, (part + 1) * width)
        return [rhs_ref[slot_at[level * LANES + m]][:, columns] for m in range(LANES)]

    solve(0, 0, rhs_of(0, 0), send_own)
    solve(0, 1, rhs_of(0, 1), lambda t, m: None)
    for level in range(1, STEPS):
        for part in range(PARTS):
            for m, block in enumerate(rhs_of(level, part)):
                acc[own_at(level, part, m)] = block
    loads[2].wait()
    lax.fori_loop(0, (STEPS - 1) * GROUPS * LANES, prepare, 0)
    sent(0)
    for m in range(LANES):
        send_own(1, m)

    def step(t, carry):
        k, part = t // PARTS, lax.rem(t, PARTS)
        ahead = k + 1
        first = k * GROUPS * LANES
        residual = [acc[own_at(ahead, part, m)] for m in range(LANES)]

        def use(entry, c, x):
            j = entry * LANES + c
            term = multiply(factor_two[first + j], x)
            terms[j] = term
            for m in range(LANES):
                residual[m] = residual[m] - weight(first + j, ahead * LANES + m) * term

        for m in range(LANES):
            use(0, m, own[own_at(k, part, m)])
        for m in range(LANES):
            take_far(t, m)
        for m in range(LANES):
            take_near(t, m)
        for entry in (4, 2):
            for m in range(LANES):
                use(entry, m, got[t, entry - 1, lane(m), :])
        for m in range(LANES):
            for entry in (1, 3):
                take_other(t, m, entry)
                use(entry, m, got[t, entry - 1, lane(m), :])

        def send(where, m):
            @pl.when(ahead < STEPS - 1)
            def _():
                if m == 0:
                    sent(where - 1)
                send_own(where, m)

        solve(ahead, part, residual, send)

        def later(level, inner):
            for m in range(LANES):
                total = acc[own_at(level, part, m)]
                for j in range(GROUPS * LANES):
                    total = total - weight(first + j, level * LANES + m) * terms[j]
                acc[own_at(level, part, m)] = total
            return inner

        lax.fori_loop(k + 2, STEPS, later, 0)
        return carry

    lax.fori_loop(0, (STEPS - 1) * PARTS, step, 0)

    sent((STEPS - 1) * PARTS - 1)

    def finish(t, carry):
        for m in range(LANES):
            for kind in range(1, 4):
                copy(t, m, kind, mine(t, m), 1, partner).wait_send()
        return carry

    lax.fori_loop(0, (STEPS - 1) * PARTS, finish, 0)
    for at in range(PARTS * slots):
        save(at).wait()


def arrange(order_ref, solved_hbm, out_hbm, sems):
    slots, _, columns = out_hbm.shape
    width = columns // PARTS
    slot_at = []
    for level in range(STEPS):
        one, two = order_ref[2 * level], order_ref[2 * level + 1]
        slot_at += [jnp.minimum(one, two), jnp.maximum(one, two)]
    copies = []
    for slot in range(slots):
        position = jnp.int32(0)
        for p in range(slots):
            position = position + p * (slot_at[p] == slot).astype(jnp.int32)
        position = jnp.minimum(position, slots - 1)
        for part in range(PARTS):
            copies.append(
                pltpu.make_async_copy(
                    solved_hbm.at[part * slots + position],
                    out_hbm.at[slot, :, pl.ds(part * width, width)],
                    sems.at[slot * PARTS + part],
                )
            )
            copies[-1].start()
    for copy in copies:
        copy.wait()


def body(rhs, diag_inv, factor_blocks, order, blk_row, blk_col):
    n = lax.axis_size("blk")
    rows, columns = rhs.shape
    size = diag_inv.shape[1]
    slots = order.shape[0]
    width = columns // PARTS
    two = LANES * size
    rounds = (STEPS - 1) * PARTS
    scratch = [
        pltpu.VMEM((slots, size, columns), F32),
        pltpu.VMEM((slots, size, size), F32),
        pltpu.VMEM(factor_blocks.shape, F32),
        pltpu.VMEM((slots, two, size), BF16),
        pltpu.VMEM((factor_blocks.shape[0], two, size), BF16),
        pltpu.SMEM((factor_blocks.shape[0],), jnp.int32),
        pltpu.VMEM((PARTS * slots, size, width), F32),
        pltpu.VMEM((PARTS * slots, size, width), F32),
        pltpu.VMEM((rounds, BAND, two, width), F32),
        pltpu.VMEM((GROUPS * LANES, size, width), F32),
        pltpu.SemaphoreType.DMA((3,)),
        pltpu.SemaphoreType.DMA((PARTS * slots,)),
        pltpu.SemaphoreType.DMA((rounds * LANES * 4,)),
        pltpu.SemaphoreType.DMA((rounds * LANES * 4,)),
    ]
    solved = pl.pallas_call(
        functools.partial(kernel, n),
        out_shape=jax.ShapeDtypeStruct((PARTS * slots, size, width), F32),
        in_specs=[pl.BlockSpec(memory_space=pltpu.SMEM)] * 3
        + [pl.BlockSpec(memory_space=pl.ANY)] * 3,
        out_specs=pl.BlockSpec(memory_space=pl.ANY),
        scratch_shapes=scratch,
        compiler_params=pltpu.CompilerParams(
            collective_id=0, has_side_effects=True, vmem_limit_bytes=56 * 1024 * 1024
        ),
        cost_estimate=pl.CostEstimate(
            flops=2 * 3 * (factor_blocks.shape[0] + slots) * size * size * columns,
            bytes_accessed=4 * (2 * rows * columns + rows * size + factor_blocks.size),
            transcendentals=0,
        ),
    )(
        order,
        blk_row,
        blk_col,
        rhs.reshape(slots, size, columns),
        diag_inv.reshape(slots, size, size),
        factor_blocks,
    )
    out = pl.pallas_call(
        arrange,
        out_shape=jax.ShapeDtypeStruct((slots, size, columns), F32),
        in_specs=[
            pl.BlockSpec(memory_space=pltpu.SMEM),
            pl.BlockSpec(memory_space=pl.ANY),
        ],
        out_specs=pl.BlockSpec(memory_space=pl.ANY),
        scratch_shapes=[pltpu.SemaphoreType.DMA((PARTS * slots,))],
        cost_estimate=pl.CostEstimate(
            flops=0, bytes_accessed=8 * rows * columns, transcendentals=0
        ),
    )(order, solved)
    return out.reshape(rows, columns)


def solution(mesh):
    placed = (P("blk", None), P("blk", None), P("blk", None, None), P("blk"), P("blk"), P("blk"))
    return jax.shard_map(
        body, mesh=mesh, in_specs=placed, out_specs=P("blk", None), check_vma=False
    )
```

```python
import functools

import jax
import jax.numpy as jnp
from jax import lax
from jax.experimental import pallas as pl
from jax.experimental.pallas import tpu as pltpu
from jax.sharding import PartitionSpec as P

LANES = 2
STEPS = 4
BAND = 4
PARTS = 2
GROUPS = BAND + 1
MESH = pl.DeviceIdType.MESH
F32 = jnp.float32
BF16 = jnp.bfloat16


def split(x):
    high = x.astype(BF16)
    return high, (x - high.astype(F32)).astype(BF16)


def dot(a, b):
    return jnp.dot(a, b, preferred_element_type=F32)


def kernel(
    n,
    order_ref,
    row_ref,
    col_ref,
    rhs_hbm,
    diag_hbm,
    factor_hbm,
    out_hbm,
    rhs_ref,
    diag_ref,
    factor_ref,
    diag_two,
    factor_two,
    where_to,
    acc,
    own,
    got,
    terms,
    load_sems,
    out_sems,
    send_sems,
    recv_sems,
):
    slots = order_ref.shape[0]
    size = diag_ref.shape[1]
    width = rhs_ref.shape[2] // PARTS
    me = lax.axis_index("blk")
    core = lax.rem(me, 2)
    chip = me // 2
    odd = lax.rem(chip, 2)
    partner = me + 1 - 2 * core
    buddy = me + 2 - 4 * odd
    above = lax.rem(me + 4, n)
    below = lax.rem(me + n - 4, n)

    loads = [
        pltpu.make_async_copy(src, dst, load_sems.at[at])
        for at, (src, dst) in enumerate(
            ((diag_hbm, diag_ref), (rhs_hbm, rhs_ref), (factor_hbm, factor_ref))
        )
    ]
    for load in loads:
        load.start()

    barrier = pltpu.get_barrier_semaphore()
    for device in (partner, buddy, below):
        pl.semaphore_signal(barrier, inc=1, device_id=(device,), device_id_type=MESH)
    pl.semaphore_wait(barrier, 3)

    slot_at = []
    for level in range(STEPS):
        one, two = order_ref[2 * level], order_ref[2 * level + 1]
        slot_at += [jnp.minimum(one, two), jnp.maximum(one, two)]

    def lane(m):
        return pl.ds(m * size, size)

    def own_at(level, part, m):
        return (part * STEPS + level) * LANES + m

    def copy(t, m, kind, src, entry, device):
        at = (t * LANES + m) * 4
        return pltpu.make_async_remote_copy(
            src_ref=src,
            dst_ref=got.at[t, entry - 1].at[lane(m)],
            send_sem=send_sems.at[at + kind],
            recv_sem=recv_sems.at[at + entry - 1],
            device_id=(device,),
            device_id_type=MESH,
        )

    def mine(t, m):
        return own.at[own_at(t // PARTS, lax.rem(t, PARTS), m)]

    def there(t, m, entry):
        return got.at[t, entry - 1].at[lane(m)]

    def send_own(t, m):
        copy(t, m, 0, mine(t, m), 4, above).start()

        @pl.when(odd == 0)
        def _():
            copy(t, m, 1, mine(t, m), 2, buddy).start()

        @pl.when(core == 0)
        def _():
            copy(t, m, 3, mine(t, m), 1, partner).start()

    def save(at):
        return pltpu.make_async_copy(own.at[at], out_hbm.at[at], out_sems.at[at])

    def take_far(t, m):
        copy(t, m, 0, mine(t, m), 4, above).wait_recv()

        @pl.when(odd == 1)
        def _():
            copy(t, m, 1, there(t, m, 4), 2, buddy).start()

        @pl.when(core == 1)
        def _():
            copy(t, m, 3, there(t, m, 4), 3, partner).start()

    def sent(t):
        for m in range(LANES):
            copy(t, m, 0, mine(t, m), 4, above).wait_send()

    def take_near(t, m):
        copy(t, m, 1, mine(t, m), 2, buddy).wait_recv()
        copy(t, m, 2, there(t, m, 2), 3 - 2 * core, partner).start()

    def take_other(t, m, entry):
        copy(t, m, 2, mine(t, m), entry, partner).wait_recv()

    def tall(x):
        return jnp.concatenate(split(x), axis=0)

    def multiply(two, x):
        every = dot(two, jnp.concatenate(split(x), axis=1))
        top = every[0:size, 0:width] + every[0:size, width:]
        return top + (every[size:, 0:width] + every[size:, width:])

    def solve(level, part, residual, send):
        t = level * PARTS + part
        for m in range(LANES):
            at = own_at(level, part, m)
            own[at] = multiply(diag_two[level * LANES + m], residual[m])
            send(t, m)
            save(at).start()

    def prepare(index, carry):
        c = lax.rem(index, LANES)
        base = index - c
        swapped = (col_ref[base] > col_ref[base + 1]).astype(jnp.int32)
        second = swapped + c - 2 * swapped * c
        factor_two[index] = tall(factor_ref[base + second])
        slot = row_ref[base] * (1 - second) + row_ref[base + 1] * second - me * slots
        position = jnp.int32(0)
        for p in range(slots):
            position = position + p * (slot_at[p] == slot).astype(jnp.int32)
        where_to[index] = position
        return carry

    def weight(j, position):
        return (where_to[j] == position).astype(jnp.int32).astype(F32)

    loads[0].wait()
    for p in range(slots):
        diag_two[p] = tall(diag_ref[slot_at[p]])
    loads[1].wait()

    def rhs_of(level, part):
        columns = slice(part * width, (part + 1) * width)
        return [rhs_ref[slot_at[level * LANES + m]][:, columns] for m in range(LANES)]

    solve(0, 0, rhs_of(0, 0), send_own)
    solve(0, 1, rhs_of(0, 1), lambda t, m: None)
    for level in range(1, STEPS):
        for part in range(PARTS):
            for m, block in enumerate(rhs_of(level, part)):
                acc[own_at(level, part, m)] = block
    loads[2].wait()
    lax.fori_loop(0, (STEPS - 1) * GROUPS * LANES, prepare, 0)
    sent(0)
    for m in range(LANES):
        send_own(1, m)

    def step(t, carry):
        k, part = t // PARTS, lax.rem(t, PARTS)
        ahead = k + 1
        first = k * GROUPS * LANES
        residual = [acc[own_at(ahead, part, m)] for m in range(LANES)]

        def use(entry, c, x):
            j = entry * LANES + c
            term = multiply(factor_two[first + j], x)
            terms[j] = term
            for m in range(LANES):
                residual[m] = residual[m] - weight(first + j, ahead * LANES + m) * term

        for m in range(LANES):
            take_far(t, m)
            take_near(t, m)
        for m in range(LANES):
            use(0, m, own[own_at(k, part, m)])
        for entry in (4, 2):
            for m in range(LANES):
                use(entry, m, got[t, entry - 1, lane(m), :])
        for m in range(LANES):
            for entry in (1, 3):
                take_other(t, m, entry)
        for m in range(LANES):
            for entry in (1, 3):
                use(entry, m, got[t, entry - 1, lane(m), :])

        def send(where, m):
            @pl.when(ahead < STEPS - 1)
            def _():
                if m == 0:
                    sent(where - 1)
                send_own(where, m)

        solve(ahead, part, residual, send)

        def later(level, inner):
            for m in range(LANES):
                total = acc[own_at(level, part, m)]
                for j in range(GROUPS * LANES):
                    total = total - weight(first + j, level * LANES + m) * terms[j]
                acc[own_at(level, part, m)] = total
            return inner

        lax.fori_loop(k + 2, STEPS, later, 0)
        return carry

    lax.fori_loop(0, (STEPS - 1) * PARTS, step, 0)

    sent((STEPS - 1) * PARTS - 1)

    def finish(t, carry):
        for m in range(LANES):
            for kind in range(1, 4):
                copy(t, m, kind, mine(t, m), 1, partner).wait_send()
        return carry

    lax.fori_loop(0, (STEPS - 1) * PARTS, finish, 0)
    for at in range(PARTS * slots):
        save(at).wait()


def arrange(order_ref, solved_ref, out_hbm, staged, sems):
    slots, _, columns = out_hbm.shape
    width = columns // PARTS
    slot_at = []
    for level in range(STEPS):
        one, two = order_ref[2 * level], order_ref[2 * level + 1]
        slot_at += [jnp.minimum(one, two), jnp.maximum(one, two)]
    copies = []
    for slot in range(slots):
        position = jnp.int32(0)
        for p in range(slots):
            position = position + p * (slot_at[p] == slot).astype(jnp.int32)
        position = jnp.minimum(position, slots - 1)
        for part in range(PARTS):
            columns_of = slice(part * width, (part + 1) * width)
            staged[slot, :, columns_of] = solved_ref[part * slots + position]
        copies.append(
            pltpu.make_async_copy(staged.at[slot], out_hbm.at[slot], sems.at[slot])
        )
        copies[-1].start()
    for copy in copies:
        copy.wait()


def body(rhs, diag_inv, factor_blocks, order, blk_row, blk_col):
    n = lax.axis_size("blk")
    rows, columns = rhs.shape
    size = diag_inv.shape[1]
    slots = order.shape[0]
    width = columns // PARTS
    two = LANES * size
    rounds = (STEPS - 1) * PARTS
    scratch = [
        pltpu.VMEM((slots, size, columns), F32),
        pltpu.VMEM((slots, size, size), F32),
        pltpu.VMEM(factor_blocks.shape, F32),
        pltpu.VMEM((slots, two, size), BF16),
        pltpu.VMEM((factor_blocks.shape[0], two, size), BF16),
        pltpu.SMEM((factor_blocks.shape[0],), jnp.int32),
        pltpu.VMEM((PARTS * slots, size, width), F32),
        pltpu.VMEM((PARTS * slots, size, width), F32),
        pltpu.VMEM((rounds, BAND, two, width), F32),
        pltpu.VMEM((GROUPS * LANES, size, width), F32),
        pltpu.SemaphoreType.DMA((3,)),
        pltpu.SemaphoreType.DMA((PARTS * slots,)),
        pltpu.SemaphoreType.DMA((rounds * LANES * 4,)),
        pltpu.SemaphoreType.DMA((rounds * LANES * 4,)),
    ]
    solved = pl.pallas_call(
        functools.partial(kernel, n),
        out_shape=jax.ShapeDtypeStruct((PARTS * slots, size, width), F32),
        in_specs=[pl.BlockSpec(memory_space=pltpu.SMEM)] * 3
        + [pl.BlockSpec(memory_space=pl.ANY)] * 3,
        out_specs=pl.BlockSpec(memory_space=pl.ANY),
        scratch_shapes=scratch,
        compiler_params=pltpu.CompilerParams(
            collective_id=0, has_side_effects=True, vmem_limit_bytes=56 * 1024 * 1024
        ),
        cost_estimate=pl.CostEstimate(
            flops=2 * 3 * (factor_blocks.shape[0] + slots) * size * size * columns,
            bytes_accessed=4 * (2 * rows * columns + rows * size + factor_blocks.size),
            transcendentals=0,
        ),
    )(
        order,
        blk_row,
        blk_col,
        rhs.reshape(slots, size, columns),
        diag_inv.reshape(slots, size, size),
        factor_blocks,
    )
    out = pl.pallas_call(
        arrange,
        out_shape=jax.ShapeDtypeStruct((slots, size, columns), F32),
        in_specs=[
            pl.BlockSpec(memory_space=pltpu.SMEM),
            pl.BlockSpec(memory_space=pltpu.VMEM),
        ],
        out_specs=pl.BlockSpec(memory_space=pl.ANY),
        scratch_shapes=[
            pltpu.VMEM((slots, size, columns), F32),
            pltpu.SemaphoreType.DMA((slots,)),
        ],
        cost_estimate=pl.CostEstimate(
            flops=0, bytes_accessed=8 * rows * columns, transcendentals=0
        ),
    )(order, solved)
    return out.reshape(rows, columns)


def solution(mesh):
    placed = (P("blk", None), P("blk", None), P("blk", None, None), P("blk"), P("blk"), P("blk"))
    return jax.shard_map(
        body, mesh=mesh, in_specs=placed, out_specs=P("blk", None), check_vma=False
    )
```

```python
import functools

import jax
import jax.numpy as jnp
from jax import lax
from jax.experimental import pallas as pl
from jax.experimental.pallas import tpu as pltpu
from jax.sharding import PartitionSpec as P

LANES = 2
STEPS = 4
BAND = 4
PARTS = 2
GROUPS = BAND + 1
MESH = pl.DeviceIdType.MESH
F32 = jnp.float32
BF16 = jnp.bfloat16


def split(x):
    high = x.astype(BF16)
    return high, (x - high.astype(F32)).astype(BF16)


def dot(a, b):
    return jnp.dot(a, b, preferred_element_type=F32)


def kernel(
    n,
    order_ref,
    row_ref,
    col_ref,
    rhs_hbm,
    diag_hbm,
    factor_hbm,
    out_hbm,
    rhs_ref,
    diag_ref,
    factor_ref,
    diag_two,
    factor_two,
    where_to,
    acc,
    own,
    got,
    terms,
    load_sems,
    out_sems,
    send_sems,
    recv_sems,
):
    slots = order_ref.shape[0]
    size = diag_ref.shape[1]
    width = rhs_ref.shape[2] // PARTS
    me = lax.axis_index("blk")
    core = lax.rem(me, 2)
    chip = me // 2
    odd = lax.rem(chip, 2)
    partner = me + 1 - 2 * core
    buddy = me + 2 - 4 * odd
    following = lax.rem(me + 2, n)
    above = lax.rem(me + 4, n)
    below = lax.rem(me + n - 4, n)

    loads = [
        pltpu.make_async_copy(src, dst, load_sems.at[at])
        for at, (src, dst) in enumerate(
            ((diag_hbm, diag_ref), (rhs_hbm, rhs_ref), (factor_hbm, factor_ref))
        )
    ]
    for load in loads:
        load.start()

    barrier = pltpu.get_barrier_semaphore()
    for device in (partner, buddy, below):
        pl.semaphore_signal(barrier, inc=1, device_id=(device,), device_id_type=MESH)

    @pl.when(odd == 0)
    def _():
        before = lax.rem(me + n - 2, n)
        pl.semaphore_signal(barrier, inc=1, device_id=(before,), device_id_type=MESH)

    pl.semaphore_wait(barrier, 3 + odd)

    slot_at = []
    for level in range(STEPS):
        one, two = order_ref[2 * level], order_ref[2 * level + 1]
        slot_at += [jnp.minimum(one, two), jnp.maximum(one, two)]

    def lane(m):
        return pl.ds(m * size, size)

    def own_at(level, part, m):
        return (part * STEPS + level) * LANES + m

    def copy(t, m, kind, src, entry, device):
        at = (t * LANES + m) * 4
        return pltpu.make_async_remote_copy(
            src_ref=src,
            dst_ref=got.at[t, entry - 1].at[lane(m)],
            send_sem=send_sems.at[at + kind],
            recv_sem=recv_sems.at[at + entry - 1],
            device_id=(device,),
            device_id_type=MESH,
        )

    def mine(t, m):
        return own.at[own_at(t // PARTS, lax.rem(t, PARTS), m)]

    def there(t, m, entry):
        return got.at[t, entry - 1].at[lane(m)]

    def send_own(t, m):
        copy(t, m, 0, mine(t, m), 4, above).start()

        if m == 0:

            @pl.when(odd == 0)
            def _():
                copy(t, m, 1, mine(t, m), 2, buddy).start()

        else:
            copy(t, m, 1, mine(t, m), 2, following).start()

        @pl.when(core == 0)
        def _():
            copy(t, m, 3, mine(t, m), 1, partner).start()

    def save(at):
        return pltpu.make_async_copy(own.at[at], out_hbm.at[at], out_sems.at[at])

    def take_far(t, m):
        copy(t, m, 0, mine(t, m), 4, above).wait_recv()

        if m == 0:

            @pl.when(odd == 1)
            def _():
                copy(t, m, 1, there(t, m, 4), 2, buddy).start()

        @pl.when(core == 1)
        def _():
            copy(t, m, 3, there(t, m, 4), 3, partner).start()

    def sent(t):
        for m in range(LANES):
            copy(t, m, 0, mine(t, m), 4, above).wait_send()

    def take_near(t, m):
        copy(t, m, 1, mine(t, m), 2, buddy).wait_recv()
        copy(t, m, 2, there(t, m, 2), 3 - 2 * core, partner).start()

    def take_other(t, m, entry):
        copy(t, m, 2, mine(t, m), entry, partner).wait_recv()

    def tall(x):
        return jnp.concatenate(split(x), axis=0)

    def multiply(two, x):
        every = dot(two, jnp.concatenate(split(x), axis=1))
        top = every[0:size, 0:width] + every[0:size, width:]
        return top + (every[size:, 0:width] + every[size:, width:])

    def solve(level, part, residual, send):
        t = level * PARTS + part
        for m in range(LANES):
            at = own_at(level, part, m)
            own[at] = multiply(diag_two[level * LANES + m], residual[m])
            send(t, m)
            save(at).start()

    def prepare(index, carry):
        c = lax.rem(index, LANES)
        base = index - c
        swapped = (col_ref[base] > col_ref[base + 1]).astype(jnp.int32)
        second = swapped + c - 2 * swapped * c
        factor_two[index] = tall(factor_ref[base + second])
        slot = row_ref[base] * (1 - second) + row_ref[base + 1] * second - me * slots
        position = jnp.int32(0)
        for p in range(slots):
            position = position + p * (slot_at[p] == slot).astype(jnp.int32)
        where_to[index] = position
        return carry

    def weight(j, position):
        return (where_to[j] == position).astype(jnp.int32).astype(F32)

    loads[0].wait()
    for p in range(slots):
        diag_two[p] = tall(diag_ref[slot_at[p]])
    loads[1].wait()

    def rhs_of(level, part):
        columns = slice(part * width, (part + 1) * width)
        return [rhs_ref[slot_at[level * LANES + m]][:, columns] for m in range(LANES)]

    solve(0, 0, rhs_of(0, 0), send_own)
    solve(0, 1, rhs_of(0, 1), lambda t, m: None)
    for level in range(1, STEPS):
        for part in range(PARTS):
            for m, block in enumerate(rhs_of(level, part)):
                acc[own_at(level, part, m)] = block
    loads[2].wait()
    lax.fori_loop(0, (STEPS - 1) * GROUPS * LANES, prepare, 0)
    sent(0)
    for m in range(LANES):
        send_own(1, m)

    def step(t, carry):
        k, part = t // PARTS, lax.rem(t, PARTS)
        ahead = k + 1
        first = k * GROUPS * LANES
        residual = [acc[own_at(ahead, part, m)] for m in range(LANES)]

        def use(entry, c, x):
            j = entry * LANES + c
            term = multiply(factor_two[first + j], x)
            terms[j] = term
            for m in range(LANES):
                residual[m] = residual[m] - weight(first + j, ahead * LANES + m) * term

        for m in range(LANES):
            take_far(t, m)
        for m in (1, 0):
            take_near(t, m)
        for m in range(LANES):
            use(0, m, own[own_at(k, part, m)])
        for entry in (4, 2):
            for m in range(LANES):
                use(entry, m, got[t, entry - 1, lane(m), :])
        for m in range(LANES):
            for entry in (1, 3):
                take_other(t, m, entry)
        for m in range(LANES):
            for entry in (1, 3):
                use(entry, m, got[t, entry - 1, lane(m), :])

        def send(where, m):
            @pl.when(ahead < STEPS - 1)
            def _():
                if m == 0:
                    sent(where - 1)
                send_own(where, m)

        solve(ahead, part, residual, send)

        def later(level, inner):
            for m in range(LANES):
                total = acc[own_at(level, part, m)]
                for j in range(GROUPS * LANES):
                    total = total - weight(first + j, level * LANES + m) * terms[j]
                acc[own_at(level, part, m)] = total
            return inner

        lax.fori_loop(k + 2, STEPS, later, 0)
        return carry

    lax.fori_loop(0, (STEPS - 1) * PARTS, step, 0)

    sent((STEPS - 1) * PARTS - 1)

    def finish(t, carry):
        for m in range(LANES):
            for kind in range(1, 4):
                copy(t, m, kind, mine(t, m), 1, partner).wait_send()
        return carry

    lax.fori_loop(0, (STEPS - 1) * PARTS, finish, 0)
    for at in range(PARTS * slots):
        save(at).wait()


def arrange(order_ref, solved_ref, out_hbm, staged, sems):
    slots, _, columns = out_hbm.shape
    width = columns // PARTS
    slot_at = []
    for level in range(STEPS):
        one, two = order_ref[2 * level], order_ref[2 * level + 1]
        slot_at += [jnp.minimum(one, two), jnp.maximum(one, two)]
    copies = []
    for slot in range(slots):
        position = jnp.int32(0)
        for p in range(slots):
            position = position + p * (slot_at[p] == slot).astype(jnp.int32)
        position = jnp.minimum(position, slots - 1)
        for part in range(PARTS):
            columns_of = slice(part * width, (part + 1) * width)
            staged[slot, :, columns_of] = solved_ref[part * slots + position]
        copies.append(
            pltpu.make_async_copy(staged.at[slot], out_hbm.at[slot], sems.at[slot])
        )
        copies[-1].start()
    for copy in copies:
        copy.wait()


def body(rhs, diag_inv, factor_blocks, order, blk_row, blk_col):
    n = lax.axis_size("blk")
    rows, columns = rhs.shape
    size = diag_inv.shape[1]
    slots = order.shape[0]
    width = columns // PARTS
    two = LANES * size
    rounds = (STEPS - 1) * PARTS
    scratch = [
        pltpu.VMEM((slots, size, columns), F32),
        pltpu.VMEM((slots, size, size), F32),
        pltpu.VMEM(factor_blocks.shape, F32),
        pltpu.VMEM((slots, two, size), BF16),
        pltpu.VMEM((factor_blocks.shape[0], two, size), BF16),
        pltpu.SMEM((factor_blocks.shape[0],), jnp.int32),
        pltpu.VMEM((PARTS * slots, size, width), F32),
        pltpu.VMEM((PARTS * slots, size, width), F32),
        pltpu.VMEM((rounds, BAND, two, width), F32),
        pltpu.VMEM((GROUPS * LANES, size, width), F32),
        pltpu.SemaphoreType.DMA((3,)),
        pltpu.SemaphoreType.DMA((PARTS * slots,)),
        pltpu.SemaphoreType.DMA((rounds * LANES * 4,)),
        pltpu.SemaphoreType.DMA((rounds * LANES * 4,)),
    ]
    solved = pl.pallas_call(
        functools.partial(kernel, n),
        out_shape=jax.ShapeDtypeStruct((PARTS * slots, size, width), F32),
        in_specs=[pl.BlockSpec(memory_space=pltpu.SMEM)] * 3
        + [pl.BlockSpec(memory_space=pl.ANY)] * 3,
        out_specs=pl.BlockSpec(memory_space=pl.ANY),
        scratch_shapes=scratch,
        compiler_params=pltpu.CompilerParams(
            collective_id=0, has_side_effects=True, vmem_limit_bytes=56 * 1024 * 1024
        ),
        cost_estimate=pl.CostEstimate(
            flops=2 * 3 * (factor_blocks.shape[0] + slots) * size * size * columns,
            bytes_accessed=4 * (2 * rows * columns + rows * size + factor_blocks.size),
            transcendentals=0,
        ),
    )(
        order,
        blk_row,
        blk_col,
        rhs.reshape(slots, size, columns),
        diag_inv.reshape(slots, size, size),
        factor_blocks,
    )
    out = pl.pallas_call(
        arrange,
        out_shape=jax.ShapeDtypeStruct((slots, size, columns), F32),
        in_specs=[
            pl.BlockSpec(memory_space=pltpu.SMEM),
            pl.BlockSpec(memory_space=pltpu.VMEM),
        ],
        out_specs=pl.BlockSpec(memory_space=pl.ANY),
        scratch_shapes=[
            pltpu.VMEM((slots, size, columns), F32),
            pltpu.SemaphoreType.DMA((slots,)),
        ],
        cost_estimate=pl.CostEstimate(
            flops=0, bytes_accessed=8 * rows * columns, transcendentals=0
        ),
    )(order, solved)
    return out.reshape(rows, columns)


def solution(mesh):
    placed = (P("blk", None), P("blk", None), P("blk", None, None), P("blk"), P("blk"), P("blk"))
    return jax.shard_map(
        body, mesh=mesh, in_specs=placed, out_specs=P("blk", None), check_vma=False
    )
```
